512 devices in a mesh: row: 16 (over x_lo, y), tm: 8 (over z), head: 4 (over x_hi, core).
Axes of the slice: x: 4 (x_hi: 2, x_lo: 2; x = x_hi * 2 + x_lo), y: 8, z: 8, core: 2. Of those that a mesh axis runs over, the one named last changes fastest.
Arguments:
- stream: bfloat16 [32, 64, 24, 3072], P('tm', 'row'), may hold values from -60 to 60
- qkv1: bfloat16 [32, 64, 24, 3, 1536], P('tm', 'row', None, None, 'head'), may hold values from -40 to 40
- w_out1: bfloat16 [3072, 1536], P(('row', 'tm'), 'head'), may hold values from -0.5 to 0.5
- gain: float32 [3072], replicated, may hold values from 0.3 to 3
- w_qkv2: bfloat16 [3072, 3, 1536], P(('row', 'tm'), None, 'head'), may hold values from -0.8 to 0.8
Outputs:
- updated: bfloat16 [32, 64, 24, 3072], P('tm', 'row', None, 'head')
- layer_two: bfloat16 [32, 64, 24, 1536], P('tm', 'row', None, 'head')
The draws below stay inside these ranges and needn't reach their ends.
All inputs are finite; a program needn't handle non-finite values.
Results may differ from the reference program's by a relative error of at most 0.033.
Values may be sent and summed in bfloat16 or wider, within the bound.
A program may use at most 64 MiB of HBM per device.

```python
import math
import jax
import jax.numpy as jnp
from jax import lax

D = 3072
HEADS = 12
HDIM = 128
WT = 4
WH = 4
WW = 8
COLS = 24
FRAMES = 32
ROWS = 64
N_HEAD = 4


def draw_stream(key, part):
    key = jax.random.fold_in(key, 11)
    key_col, key_row, key_base = jax.random.split(key, 3)
    full_shape = (FRAMES, ROWS, COLS, D)
    col_scale = jnp.exp(jax.random.uniform(key_col, (D,), jnp.float32, 0.0, math.log(10.0)))
    row_scale = jnp.exp(jax.random.uniform(key_row, (FRAMES, ROWS, COLS, 1), jnp.float32, 0.0, math.log(10.0)))
    basic_draw = jnp.clip(jax.random.normal(key_base, full_shape, jnp.float32), -6.0, 6.0)
    return (0.1 * basic_draw * col_scale * row_scale).astype(jnp.bfloat16)


def draw_qkv1(key, part):
    key = jax.random.fold_in(key, 12)
    key_base = jax.random.fold_in(key, 0)
    full_shape = (FRAMES, ROWS, COLS, 3, HEADS * HDIM)
    stacked = jnp.clip(jax.random.normal(key_base, full_shape, jnp.float32), -5.0, 5.0)
    return stacked.astype(jnp.bfloat16)


def draw_w_qkv2(key, part):
    key = jax.random.fold_in(key, 13)
    key_base = jax.random.fold_in(key, 0)
    full_shape = (D, 3, HEADS * HDIM)
    stacked = 0.02 * jnp.clip(jax.random.normal(key_base, full_shape, jnp.float32), -6.0, 6.0)
    return stacked.astype(jnp.bfloat16)


def shard_levels(rng, dims, shards, least, top_value):
    level = 1.0
    for position, blocks in shards:
        draws = jax.random.uniform(jax.random.fold_in(jax.random.fold_in(rng, 6), position), (blocks,), jnp.float32, least / len(shards), top_value / len(shards))
        level = level * jnp.repeat(jnp.exp(draws), dims[position] // blocks).reshape((-1,) + (1,) * (len(dims) - 1 - position))
    return level


def noise(rng, extent, deviation, bound, cuts=(), held_as=jnp.bfloat16):
    loudness = shard_levels(rng, extent, cuts, -0.22, 0.18) if cuts else 1.0
    drawn = jax.random.normal(rng, extent, jnp.float32) * deviation * loudness
    return jnp.minimum(jnp.maximum(drawn, -bound), bound).astype(held_as)


def setup_inputs(seed: int = 0) -> dict:
    key_of = jax.random.split(jax.random.key(seed), 6)
    stream = draw_stream(jax.random.fold_in(key_of[5], 71), 0)
    qkv1 = draw_qkv1(jax.random.fold_in(key_of[5], 71), 0)
    w_out1 = noise(key_of[2], (D, HEADS * HDIM), HDIM ** -0.5, 0.5, ((0, 128), (1, 4)))
    gain = jnp.clip(jnp.exp(jax.random.uniform(key_of[3], (D,), jnp.float32, math.log(0.3), math.log(3.0))), 0.3, 3.0)
    w_qkv2 = draw_w_qkv2(jax.random.fold_in(key_of[5], 71), 0)
    return dict(stream=stream, qkv1=qkv1, w_out1=w_out1, gain=gain, w_qkv2=w_qkv2)


EPSILON = 1e-06

def windows(array, head_count):
    frames, tile_rows, tile_cols = (array.shape[0], array.shape[1], array.shape[2])
    array = array.reshape(frames // WT, WT, tile_rows // WH, WH, tile_cols // WW, WW, head_count, HDIM)
    array = array.transpose(0, 2, 4, 6, 1, 3, 5, 7)
    return array.reshape(-1, head_count, WT * WH * WW, HDIM)

def unwindow(array, frames, tile_rows, tile_cols):
    head_count = array.shape[1]
    array = array.reshape(frames // WT, tile_rows // WH, tile_cols // WW, head_count, WT, WH, WW, HDIM)
    array = array.transpose(0, 4, 1, 5, 2, 6, 3, 7)
    return array.reshape(frames, tile_rows, tile_cols, head_count * HDIM)

def attend(query, keys, values):
    frames, tile_rows, tile_cols, channels = query.shape
    head_count = channels // HDIM
    query_w = windows(query, head_count).astype(jnp.float32)
    keys_w = windows(keys, head_count).astype(jnp.float32)
    values_w = windows(values, head_count).astype(jnp.float32)
    scores = jnp.einsum('nhqd,nhkd->nhqk', query_w, keys_w) * HDIM ** (-0.5)
    largest = lax.optimization_barrier(jnp.max(scores, axis=-1, keepdims=True))
    weights = jnp.exp(scores - largest)
    probabilities = (weights / lax.optimization_barrier(jnp.sum(weights, axis=-1, keepdims=True))).astype(jnp.bfloat16)
    attended = jnp.einsum('nhqk,nhkd->nhqd', probabilities.astype(jnp.float32), values_w).astype(jnp.bfloat16)
    return unwindow(attended, frames, tile_rows, tile_cols)

def attend_all(query, keys, values):
    frames = query.shape[0]

    def regroup(array):
        return array.reshape((frames // WT, WT) + array.shape[1:])

    def one_group(members):
        return attend(members[0], members[1], members[2])
    results = lax.map(one_group, (regroup(query), regroup(keys), regroup(values)))
    return results.reshape((frames,) + results.shape[2:])

def reference(stream, qkv1, w_out1, gain, w_qkv2):
    layer_one = attend_all(qkv1[..., 0, :], qkv1[..., 1, :], qkv1[..., 2, :])
    flat_one = layer_one.reshape(-1, HEADS * HDIM)
    group_width = HEADS * HDIM // N_HEAD
    summed_total = jnp.zeros((flat_one.shape[0], D), jnp.float32)
    for member in range(N_HEAD):
        columns = slice(member * group_width, (member + 1) * group_width)
        partial_value = jnp.dot(flat_one[:, columns], w_out1[:, columns].T, preferred_element_type=jnp.float32)
        rounded = lax.optimization_barrier(partial_value.astype(jnp.bfloat16))
        summed_total = summed_total + rounded.astype(jnp.float32)
    updated = (stream.reshape(-1, D).astype(jnp.float32) + summed_total).astype(jnp.bfloat16)
    values = updated.astype(jnp.float32)
    meansq = lax.optimization_barrier(jnp.mean(values * values, axis=-1, keepdims=True))
    normed = (values * lax.rsqrt(meansq + EPSILON) * gain).astype(jnp.bfloat16)
    projected = jnp.dot(normed, w_qkv2.reshape(D, 3 * HEADS * HDIM), preferred_element_type=jnp.float32).astype(jnp.bfloat16)
    projected = projected.reshape(FRAMES, ROWS, COLS, 3, HEADS * HDIM)
    shifted = jnp.roll(projected, (-(WT // 2), -(WH // 2)), axis=(0, 1))
    attended = attend_all(shifted[..., 0, :], shifted[..., 1, :], shifted[..., 2, :])
    layer_two = jnp.roll(attended, (WT // 2, WH // 2), axis=(0, 1))
    return (updated.reshape(FRAMES, ROWS, COLS, D), layer_two)
```

```python
import jax
import jax.numpy as jnp
from jax import lax
from jax.experimental import pallas as pl
from jax.experimental.pallas import tpu as pltpu
from jax.sharding import PartitionSpec as P

MESH = pl.DeviceIdType.MESH
HDIM = 128
EPSILON = 1e-06
TOKENS = 384
SHARE = 768
GROUP = 384
WIDE = 1152
CHUNKS = 2
PART = TOKENS // CHUNKS
BF = jnp.bfloat16
F32 = jnp.float32

FIRST = (0, 8)
SECOND = (16, 32)
PAIR = 48
CORE_PART = 49
SUM_X = 51
SHARE_X = SUM_X + CHUNKS
SHARE_CORE = SHARE_X + CHUNKS
RELAY = SHARE_CORE + CHUNKS
HALO = RELAY + CHUNKS
BACK = HALO + 3
N_SEM = BACK + 3


def softmax_attend(q, k, v):
    scores = lax.dot_general(
        q, k, (((1,), (1,)), ((), ())), preferred_element_type=F32
    ) * HDIM ** (-0.5)
    largest = jnp.max(scores, axis=-1, keepdims=True)
    weights = jnp.exp(scores - largest)
    probabilities = (weights / jnp.sum(weights, axis=-1, keepdims=True)).astype(BF)
    return jnp.dot(probabilities, v, preferred_element_type=F32)


def kernel(
    qw, wo, wq, gain, stream, upd_out, two_out,
    own, other, ga, gb, w1, w2, l1f, l1, ps, pr, qs, xr, xf, st, ub, nb, acc, pj, hq, x2, o2, ob, lb,
    ssem, rsem, lsem,
):
    row = lax.axis_index("row")
    z = lax.axis_index("tm")
    head = lax.axis_index("head")
    xl, y = row // 8, row % 8
    xh, c = head // 2, head % 2

    def first(d):
        return (xl * 8 + (y + c * (d + 8)) % 8, (z + (1 - c) * (d + 8)) % 8, head)

    def second(d):
        return (xl * 8 + (y + (1 - c) * (d + 8)) % 8, (z + c * (d + 8)) % 8, head)

    p0 = (1 - c) * z + c * y
    s0 = (1 - c) * y + c * z
    pair_dev = ((row + 8) % 16, z, head)
    core_dev = (row, z, xh * 2 + (1 - c))
    x_dev = (row, z, (head + 2) % 4)
    row_m, row_p = (row + 15) % 16, (row + 1) % 16
    z_m, z_p = (z + 7) % 8, (z + 1) % 8
    halo_to = ((row_m, z, head), (row, z_m, head), (row_m, z_m, head))
    halo_from = ((row_p, z, head), (row, z_p, head), (row_p, z_p, head))

    barrier = pltpu.get_barrier_semaphore()
    greet = (first(1), first(-1), second(1), second(-1), pair_dev, core_dev, x_dev) + halo_to + halo_from
    for device in greet:
        pl.semaphore_signal(barrier, inc=1, device_id=device, device_id_type=MESH)
    pl.semaphore_wait(barrier, len(greet))

    sent = []

    def send(src, dst, k, device):
        copy = pltpu.make_async_remote_copy(
            src_ref=src, dst_ref=dst, send_sem=ssem.at[k], recv_sem=rsem.at[k],
            device_id=device, device_id_type=MESH,
        )
        copy.start()
        sent.append(copy)

    def arrive(dst, k, device):
        pltpu.make_async_remote_copy(
            src_ref=dst, dst_ref=dst, send_sem=ssem.at[k], recv_sem=rsem.at[k],
            device_id=device, device_id_type=MESH,
        ).wait_recv()

    stream_in = pltpu.make_async_copy(
        stream.at[:, pl.ds(pl.multiple_of(head * SHARE, SHARE), SHARE)], st, lsem.at[0]
    )
    stream_in.start()

    mine = jnp.concatenate([wo[...].astype(F32), wq[...].astype(F32)], axis=1)
    own[...] = jnp.concatenate([mine, jnp.zeros((8, GROUP + WIDE), F32)], axis=0).astype(BF)
    send(own, other, PAIR, pair_dev)

    def attend_one(w):
        def unit(h, carry):
            def lanes(part):
                return pl.ds(pl.multiple_of(part * GROUP + h * HDIM, HDIM), HDIM)

            out = softmax_attend(qw[w, :, lanes(0)], qw[w, :, lanes(1)], qw[w, :, lanes(2)])
            l1f[:, pl.ds(w * 8, 8), lanes(0)] = out.reshape(16, 8, HDIM)
            return carry

        lax.fori_loop(0, 3, unit, 0)

    attend_one(0)
    arrive(other, PAIR, pair_dev)
    theirs = other[...].astype(F32)[:24]
    pair = jnp.concatenate(
        [jnp.where(xl == 0, mine, theirs), jnp.where(xl == 0, theirs, mine)], axis=0
    ).astype(BF)
    here = s0 * 8 + p0
    ga[here] = pair[:, :GROUP]
    gb[here] = pair[:, GROUP:]
    bufs = (ga, gb)

    def first_send(a, d, hop):
        slot = bufs[a].at[s0 * 8 + (p0 + (1 - 2 * d) * (1 - hop) + 8) % 8]
        send(slot, slot, FIRST[a] + d * 4 + hop - 1, first(1 - 2 * d))

    def first_step(a, hop):
        for d in range(2):
            if hop == 4 and d != a:
                continue
            slot = bufs[a].at[s0 * 8 + (p0 - (1 - 2 * d) * hop + 8) % 8]
            arrive(slot, FIRST[a] + d * 4 + hop - 1, first(2 * d - 1))
            if hop < 3 or (hop == 3 and d == a):
                first_send(a, d, hop + 1)

    def second_slot(a, s, q):
        return bufs[a].at[pl.ds(pl.multiple_of(s * 8 + q * 4, 4), 4)]

    def second_send(a, d, hop, q):
        slot = second_slot(a, (s0 + (1 - 2 * d) * (1 - hop) + 8) % 8, q)
        send(slot, slot, SECOND[a] + d * 8 + (hop - 1) * 2 + q, second(1 - 2 * d))

    def second_start(a):
        for q in range(2):
            for d in range(2):
                second_send(a, d, 1, q)

    def second_step(a, hop, q):
        for d in range(2):
            if hop == 4 and d != q:
                continue
            slot = second_slot(a, (s0 - (1 - 2 * d) * hop + 8) % 8, q)
            arrive(slot, SECOND[a] + d * 8 + (hop - 1) * 2 + q, second(2 * d - 1))
            if hop < 3 or (hop == 3 and d == q):
                second_send(a, d, hop + 1, q)

    outs = (w1, w2)
    m0, odd = s0 // 2, s0 % 2
    ready = (m0, (m0 + 3 + 2 * odd) % 4, (m0 + 1 + 2 * odd) % 4, (m0 + 2) % 4)

    def natural(a, hop):
        m = ready[hop - 1]
        src, dst = bufs[a], outs[a]

        def body(i, carry):
            one = 16 * m + (1 - c) * 2 * i + c * i
            two = one + 1 + 7 * c
            at = (1 - c) * (8 * m + i) + c * (4 * i + m)
            g0, g1 = src[one].astype(F32), src[two].astype(F32)
            rows = pl.ds(pl.multiple_of((at % 16) * 48, 48), 48)
            dst[at // 16, rows] = jnp.concatenate([g0[:24], g1[:24]], axis=0).astype(BF)
            dst[2 + at // 16, rows] = jnp.concatenate([g0[24:], g1[24:]], axis=0).astype(BF)
            return carry

        lax.fori_loop(0, 8, body, 0)

    for a in range(2):
        for d in range(2):
            first_send(a, d, 1)
    attend_one(1)
    first_step(0, 1)
    first_step(1, 1)
    attend_one(2)
    l1[...] = l1f[...].reshape(TOKENS, GROUP).astype(BF)
    for hop in range(2, 4):
        first_step(0, hop)
        first_step(1, hop)
    first_step(0, 4)
    second_start(0)
    first_step(1, 4)
    for hop in range(1, 4):
        for q in range(2):
            second_step(0, hop, q)
        if hop == 3:
            second_start(1)
        natural(0, hop)
    for q in range(2):
        second_step(0, 4, q)
    natural(0, 4)

    def partial(share, rows, n):
        return lax.dot_general(
            l1[rows], w1[share, n * 256 : (n + 1) * 256], (((1,), (1,)), ((), ())),
            preferred_element_type=F32,
        )

    everything = slice(0, TOKENS)
    for i, far in enumerate((1 - xh, xh)):
        for n in range(3):
            ps[i, :, n * 256 : (n + 1) * 256] = partial(far * 2 + 1 - c, everything, n).astype(BF)
        send(ps.at[i], pr.at[i], CORE_PART + i, core_dev)
    arrive(pr.at[0], CORE_PART, core_dev)
    for k in range(CHUNKS):
        rows = slice(k * PART, (k + 1) * PART)
        for n in range(3):
            cols = slice(n * 256, (n + 1) * 256)
            both = partial((1 - xh) * 2 + c, rows, n) + pr[0, rows, cols].astype(F32)
            qs[rows, cols] = both.astype(BF)
        send(qs.at[pl.ds(k * PART, PART)], xr.at[pl.ds(k * PART, PART)], SUM_X + k, x_dev)
    stream_in.wait()
    arrive(pr.at[1], CORE_PART + 1, core_dev)
    for n in range(3):
        cols = slice(n * 256, (n + 1) * 256)
        xf[:, cols] = partial(head, everything, n) + pr[1, :, cols].astype(F32) + st[:, cols].astype(F32)

    def take_sum(k):
        rows = pl.ds(k * PART, PART)
        arrive(xr.at[rows], SUM_X + k, x_dev)
        ub[head, rows] = (xf[rows] + xr[rows].astype(F32)).astype(BF)
        send(ub.at[head, rows], ub.at[head, rows], SHARE_X + k, x_dev)
        send(ub.at[head, rows], ub.at[head, rows], SHARE_CORE + k, core_dev)

    far_head = (head + 2) % 4
    near_head = xh * 2 + 1 - c
    last_head = (near_head + 2) % 4

    def relay(k):
        rows = pl.ds(k * PART, PART)
        arrive(ub.at[far_head, rows], SHARE_X + k, x_dev)
        send(ub.at[far_head, rows], ub.at[far_head, rows], RELAY + k, core_dev)

    def norm(k):
        rows = pl.ds(k * PART, PART)
        arrive(ub.at[near_head, rows], SHARE_CORE + k, core_dev)
        arrive(ub.at[last_head, rows], RELAY + k, core_dev)

        def body(i, carry):
            r = pl.ds(pl.multiple_of(k * PART + i * 16, 16), 16)
            values = [ub[j, r].astype(F32) for j in range(4)]
            total = sum(jnp.sum(v * v, axis=-1, keepdims=True) for v in values)
            scale = lax.rsqrt(total / (4 * SHARE) + EPSILON)
            for j in range(4):
                nb[j, r] = (values[j] * scale * gain[j]).astype(BF)
            return carry

        lax.fori_loop(0, PART // 16, body, 0)

    second_step(1, 1, 0)
    second_step(1, 1, 1)
    natural(1, 1)
    take_sum(0)
    second_step(1, 2, 0)
    take_sum(1)
    upd = pltpu.make_async_copy(ub.at[head], upd_out, lsem.at[1])
    upd.start()
    second_step(1, 2, 1)
    natural(1, 2)
    relay(0)
    second_step(1, 3, 0)
    relay(1)
    second_step(1, 3, 1)
    natural(1, 3)
    norm(0)
    norm(1)
    second_step(1, 4, 0)
    second_step(1, 4, 1)
    natural(1, 4)

    for n in range(3):
        cols = slice(n * GROUP, (n + 1) * GROUP)
        acc[:, cols] = jnp.dot(nb[0], w2[0, :, cols], preferred_element_type=F32)

        def add(j, carry):
            acc[:, cols] += jnp.dot(nb[j], w2[j, :, cols], preferred_element_type=F32)
            return carry

        lax.fori_loop(1, 4, add, 0)
    for fh in range(2):
        for f in range(2):
            for rh in range(2):
                at = ((fh * 2 + f) * 2 + rh) * 48
                pj[fh, f, rh] = acc[at : at + 48].astype(BF)

    quarters = ((1, 0), (0, 1), (0, 0))
    for i, (fh, rh) in enumerate(quarters):
        send(pj.at[fh, :, rh], hq.at[i], HALO + i, halo_to[i])

    def place(value, fh, rh):
        for f in range(2):
            at = (fh * 2 + f) * 4 + rh * 2
            x2[at : at + 2] = value[f].astype(F32).reshape(2, 24, WIDE)

    place(pj[1, :, 1], 0, 0)
    for i, (fh, rh) in enumerate(quarters):
        arrive(hq.at[i], HALO + i, halo_from[i])
        place(hq[i], 1 - fh, 1 - rh)

    for w in range(3):
        for h in range(3):
            def window(part):
                lanes = slice(part * GROUP + h * HDIM, part * GROUP + (h + 1) * HDIM)
                return x2[:, w * 8 : w * 8 + 8, lanes].reshape(128, HDIM).astype(BF)

            out = softmax_attend(window(0), window(1), window(2))
            o2[:, w * 8 : w * 8 + 8, h * HDIM : (h + 1) * HDIM] = out.reshape(16, 8, HDIM)

    def result(fh, f, rh):
        at = (fh * 2 + f) * 4 + rh * 2
        return o2[at : at + 2].reshape(48, GROUP).astype(BF)

    for i, (fh, rh) in enumerate(quarters):
        for f in range(2):
            ob[1 - fh, f, 1 - rh] = result(1 - fh, f, 1 - rh)
        send(ob.at[1 - fh, :, 1 - rh], lb.at[fh, :, rh], BACK + i, halo_from[i])
    for f in range(2):
        lb[1, f, 1] = result(0, f, 0)
    for i, (fh, rh) in enumerate(quarters):
        arrive(lb.at[fh, :, rh], BACK + i, halo_to[i])
    two = pltpu.make_async_copy(lb, two_out, lsem.at[2])
    two.start()
    for copy in sent:
        copy.wait_send()
    upd.wait()
    two.wait()


def shards(stream, qkv1, w_out1, gain, w_qkv2):
    frames, tile_rows, tile_cols, channels = stream.shape
    windowed = qkv1.reshape(16, 3, 8, WIDE).transpose(1, 0, 2, 3).reshape(3, 128, WIDE)
    vmem = pl.BlockSpec(memory_space=pltpu.VMEM)
    anywhere = pl.BlockSpec(memory_space=pl.ANY)
    updated, layer_two = pl.pallas_call(
        kernel,
        name="layers",
        out_shape=(
            jax.ShapeDtypeStruct((TOKENS, SHARE), BF),
            jax.ShapeDtypeStruct((2, 2, 2, 48, GROUP), BF),
        ),
        in_specs=[vmem, vmem, vmem, vmem, anywhere],
        out_specs=(anywhere, anywhere),
        scratch_shapes=[
            pltpu.VMEM((32, GROUP + WIDE), BF),
            pltpu.VMEM((32, GROUP + WIDE), BF),
            pltpu.VMEM((64, 48, GROUP), BF),
            pltpu.VMEM((64, 48, WIDE), BF),
            pltpu.VMEM((4, SHARE, GROUP), BF),
            pltpu.VMEM((4, SHARE, WIDE), BF),
            pltpu.VMEM((16, 24, GROUP), F32),
            pltpu.VMEM((TOKENS, GROUP), BF),
            pltpu.VMEM((2, TOKENS, SHARE), BF),
            pltpu.VMEM((2, TOKENS, SHARE), BF),
            pltpu.VMEM((TOKENS, SHARE), BF),
            pltpu.VMEM((TOKENS, SHARE), BF),
            pltpu.VMEM((TOKENS, SHARE), F32),
            pltpu.VMEM((TOKENS, SHARE), BF),
            pltpu.VMEM((4, TOKENS, SHARE), BF),
            pltpu.VMEM((4, TOKENS, SHARE), BF),
            pltpu.VMEM((TOKENS, WIDE), F32),
            pltpu.VMEM((2, 2, 2, 48, WIDE), BF),
            pltpu.VMEM((3, 2, 48, WIDE), BF),
            pltpu.VMEM((16, 24, WIDE), F32),
            pltpu.VMEM((16, 24, GROUP), F32),
            pltpu.VMEM((2, 2, 2, 48, GROUP), BF),
            pltpu.VMEM((2, 2, 2, 48, GROUP), BF),
            pltpu.SemaphoreType.DMA((N_SEM,)),
            pltpu.SemaphoreType.DMA((N_SEM,)),
            pltpu.SemaphoreType.DMA((3,)),
        ],
        compiler_params=pltpu.CompilerParams(
            collective_id=0, has_side_effects=True, vmem_limit_bytes=56 * 2**20
        ),
    )(
        windowed,
        w_out1,
        w_qkv2.reshape(24, WIDE),
        gain.reshape(4, 1, SHARE),
        stream.reshape(TOKENS, channels),
    )
    return (
        updated.reshape(frames, tile_rows, tile_cols, SHARE),
        layer_two.reshape(frames, tile_rows, tile_cols, GROUP),
    )


def solution(mesh):
    in_specs = (
        P("tm", "row", None, None),
        P("tm", "row", None, None, "head"),
        P(("row", "tm"), "head"),
        P(),
        P(("row", "tm"), None, "head"),
    )
    out_specs = (P("tm", "row", None, "head"), P("tm", "row", None, "head"))
    return jax.shard_map(shards, mesh=mesh, in_specs=in_specs, out_specs=out_specs, check_vma=False)
```

```python
import jax
import jax.numpy as jnp
from jax import lax
from jax.experimental import pallas as pl
from jax.experimental.pallas import tpu as pltpu
from jax.sharding import PartitionSpec as P

MESH = pl.DeviceIdType.MESH
HDIM = 128
EPSILON = 1e-06
TOKENS = 384
SHARE = 768
GROUP = 384
WIDE = 1152
CHUNKS = 2
PART = TOKENS // CHUNKS
BF = jnp.bfloat16
F32 = jnp.float32

FIRST = (0, 8)
SECOND = (16, 32)
PAIR = 48
LINE = 49
LAYER_ONE = 52
CORE_PART = 53
SHARE_X = 54
SHARE_CORE = SHARE_X + CHUNKS
RELAY = SHARE_CORE + CHUNKS
HALO = RELAY + CHUNKS
BACK = HALO + 9
N_SEM = BACK + 9


def softmax_attend(q, k, v):
    scores = lax.dot_general(
        q, k, (((1,), (1,)), ((), ())), preferred_element_type=F32
    ) * HDIM ** (-0.5)
    largest = jnp.max(scores, axis=-1, keepdims=True)
    weights = jnp.exp(scores - largest)
    probabilities = (weights / jnp.sum(weights, axis=-1, keepdims=True)).astype(BF)
    return jnp.dot(probabilities, v, preferred_element_type=F32)


def kernel(
    qkv, wo, wq, gain, stream, upd_out, two_out,
    own, other, line, ga, gb, w1, w2, x1, l1f, l1, ps, pr, xf, st, ub, nb, pj, hq, x2, o2, ob, lb,
    ssem, rsem, lsem,
):
    row = lax.axis_index("row")
    z = lax.axis_index("tm")
    head = lax.axis_index("head")
    xl, y = row // 8, row % 8
    xh, c = head // 2, head % 2

    def first(d):
        return (xl * 8 + (y + c * (d + 8)) % 8, (z + (1 - c) * (d + 8)) % 8, head)

    def second(d):
        return (xl * 8 + (y + (1 - c) * (d + 8)) % 8, (z + c * (d + 8)) % 8, head)

    p0 = (1 - c) * z + c * y
    s0 = (1 - c) * y + c * z
    pair_dev = ((row + 8) % 16, z, head)
    core_dev = (row, z, xh * 2 + (1 - c))
    x_dev = (row, z, (head + 2) % 4)
    cross_dev = ((row + 8) % 16, z, (head + 2) % 4)
    row_m, row_p = (row + 15) % 16, (row + 1) % 16
    z_m, z_p = (z + 7) % 8, (z + 1) % 8
    lower = ((row_m, z, head), (row, z_m, head), (row_m, z_m, head))
    upper = ((row_p, z, head), (row, z_p, head), (row_p, z_p, head))

    barrier = pltpu.get_barrier_semaphore()
    greet = (first(1), first(-1), second(1), second(-1), pair_dev, core_dev, x_dev, cross_dev) + lower + upper
    for device in greet:
        pl.semaphore_signal(barrier, inc=1, device_id=device, device_id_type=MESH)
    pl.semaphore_wait(barrier, len(greet))

    sent = []

    def send(src, dst, k, device):
        copy = pltpu.make_async_remote_copy(
            src_ref=src, dst_ref=dst, send_sem=ssem.at[k], recv_sem=rsem.at[k],
            device_id=device, device_id_type=MESH,
        )
        copy.start()
        sent.append(copy)

    def arrive(dst, k, device):
        pltpu.make_async_remote_copy(
            src_ref=dst, dst_ref=dst, send_sem=ssem.at[k], recv_sem=rsem.at[k],
            device_id=device, device_id_type=MESH,
        ).wait_recv()

    at_x = xh * 2 + xl
    tail = jnp.zeros((8, GROUP), F32)
    line[at_x] = jnp.concatenate([wo[...].astype(F32), tail], axis=0).astype(BF)
    for i, device in enumerate((pair_dev, x_dev, cross_dev)):
        send(line.at[at_x], line.at[at_x], LINE + i, device)
    mine = jnp.concatenate(
        [wq[part, :, h * HDIM : (h + 1) * HDIM].astype(F32) for h in range(3) for part in range(3)], axis=1
    )
    own[...] = jnp.concatenate([mine, jnp.zeros((8, WIDE), F32)], axis=0).astype(BF)
    send(own, other, PAIR, pair_dev)

    stream_in = pltpu.make_async_copy(
        stream.at[:, pl.ds(pl.multiple_of(head * SHARE, SHARE), SHARE)], st, lsem.at[0]
    )
    stream_in.start()

    def widen(i, carry):
        for part in range(3):
            x1[part, i] = qkv[i, part].astype(F32)
        return carry

    lax.fori_loop(0, 16, widen, 0)

    def attend_one(w):
        def unit(h, carry):
            lanes = pl.ds(pl.multiple_of(h * HDIM, HDIM), HDIM)

            def window(part):
                return x1[part, :, w * 8 : w * 8 + 8, lanes].reshape(128, HDIM).astype(BF)

            out = softmax_attend(window(0), window(1), window(2))
            l1f[:, w * 8 : w * 8 + 8, lanes] = out.reshape(16, 8, HDIM)
            return carry

        lax.fori_loop(0, 3, unit, 0)

    def at_line(flip_low, flip_high):
        return (xh + flip_high * (1 - 2 * xh)) * 2 + xl + flip_low * (1 - 2 * xl)

    arrive(line.at[at_line(1, 0)], LINE, pair_dev)
    arrive(line.at[at_line(0, 1)], LINE + 1, x_dev)
    arrive(line.at[at_line(1, 1)], LINE + 2, cross_dev)
    here = s0 * 8 + p0
    ga[here] = jnp.concatenate(
        [line[xh].astype(F32)[:24], line[2 + xh].astype(F32)[:24]], axis=0
    ).astype(BF)
    bufs = (ga, gb)

    def first_send(a, d, hop):
        slot = bufs[a].at[s0 * 8 + (p0 + (1 - 2 * d) * (1 - hop) + 8) % 8]
        send(slot, slot, FIRST[a] + d * 4 + hop - 1, first(1 - 2 * d))

    def first_step(a, hop):
        for d in range(2):
            if hop == 4 and d != a:
                continue
            slot = bufs[a].at[s0 * 8 + (p0 - (1 - 2 * d) * hop + 8) % 8]
            arrive(slot, FIRST[a] + d * 4 + hop - 1, first(2 * d - 1))
            if hop < 3 or (hop == 3 and d == a):
                first_send(a, d, hop + 1)

    def second_slot(a, s, q):
        return bufs[a].at[pl.ds(pl.multiple_of(s * 8 + q * 4, 4), 4)]

    def second_send(a, d, hop, q):
        slot = second_slot(a, (s0 + (1 - 2 * d) * (1 - hop) + 8) % 8, q)
        send(slot, slot, SECOND[a] + d * 8 + (hop - 1) * 2 + q, second(1 - 2 * d))

    def second_start(a, q):
        for d in range(2):
            second_send(a, d, 1, q)

    def second_step(a, hop, q):
        for d in range(2):
            if hop == 4 and d != q:
                continue
            slot = second_slot(a, (s0 - (1 - 2 * d) * hop + 8) % 8, q)
            arrive(slot, SECOND[a] + d * 8 + (hop - 1) * 2 + q, second(2 * d - 1))
            if hop < 3 or (hop == 3 and d == q):
                second_send(a, d, hop + 1, q)

    outs = (w1, w2)
    m0, odd = s0 // 2, s0 % 2
    ready = (m0, (m0 + 3 + 2 * odd) % 4, (m0 + 1 + 2 * odd) % 4, (m0 + 2) % 4)

    def natural(a, hop):
        m = ready[hop - 1]
        src, dst = bufs[a], outs[a]

        def body(i, carry):
            one = 16 * m + (1 - c) * 2 * i + c * i
            two = one + 1 + 7 * c
            at = (1 - c) * (8 * m + i) + c * (4 * i + m)
            g0, g1 = src[one].astype(F32), src[two].astype(F32)
            rows = pl.ds(pl.multiple_of(at * 48, 48), 48)
            dst[0, rows] = jnp.concatenate([g0[:24], g1[:24]], axis=0).astype(BF)
            dst[1, rows] = jnp.concatenate([g0[24:], g1[24:]], axis=0).astype(BF)
            return carry

        lax.fori_loop(0, 8, body, 0)

    for d in range(2):
        first_send(0, d, 1)
    arrive(other, PAIR, pair_dev)
    theirs = other[...].astype(F32)[:24]
    gb[here] = jnp.concatenate(
        [jnp.where(xl == 0, mine, theirs), jnp.where(xl == 0, theirs, mine)], axis=0
    ).astype(BF)
    for d in range(2):
        first_send(1, d, 1)
    attend_one(0)
    first_step(0, 1)
    first_step(1, 1)
    attend_one(1)
    first_step(0, 2)
    first_step(1, 2)
    attend_one(2)
    first_step(0, 3)
    first_step(1, 3)
    l1[xh] = l1f[...].reshape(TOKENS, GROUP).astype(BF)
    send(l1.at[xh], l1.at[xh], LAYER_ONE, x_dev)
    first_step(0, 4)
    second_start(0, 0)
    second_start(0, 1)
    first_step(1, 4)
    second_start(1, 0)
    second_step(0, 1, 0)
    second_step(0, 1, 1)
    second_start(1, 1)
    second_step(0, 2, 0)
    second_step(0, 2, 1)
    natural(0, 1)
    second_step(1, 1, 0)
    second_step(0, 3, 0)
    second_step(0, 3, 1)
    natural(0, 2)
    second_step(1, 1, 1)
    natural(0, 3)
    second_step(0, 4, 0)
    second_step(0, 4, 1)
    natural(0, 4)

    arrive(l1.at[1 - xh], LAYER_ONE, x_dev)

    def partial(share, n):
        rows = pl.ds(pl.multiple_of(share * SHARE + n * 256, 256), 256)
        return sum(
            lax.dot_general(
                l1[j], w1[j, rows], (((1,), (1,)), ((), ())), preferred_element_type=F32
            )
            for j in range(2)
        )

    for n in range(3):
        ps[:, n * 256 : (n + 1) * 256] = partial(1 - c, n).astype(BF)
    send(ps, pr, CORE_PART, core_dev)
    stream_in.wait()
    for n in range(3):
        cols = slice(n * 256, (n + 1) * 256)
        xf[:, cols] = partial(c, n) + st[:, cols].astype(F32)
    arrive(pr, CORE_PART, core_dev)
    for k in range(CHUNKS):
        rows = pl.ds(k * PART, PART)
        ub[head, rows] = (xf[rows] + pr[rows].astype(F32)).astype(BF)
        send(ub.at[head, rows], ub.at[head, rows], SHARE_X + k, x_dev)
        send(ub.at[head, rows], ub.at[head, rows], SHARE_CORE + k, core_dev)
    upd = pltpu.make_async_copy(ub.at[head], upd_out, lsem.at[1])
    upd.start()

    far_head = (head + 2) % 4
    near_head = xh * 2 + 1 - c
    last_head = (near_head + 2) % 4

    def relay(k):
        rows = pl.ds(k * PART, PART)
        arrive(ub.at[far_head, rows], SHARE_X + k, x_dev)
        send(ub.at[far_head, rows], ub.at[far_head, rows], RELAY + k, core_dev)

    def norm(k):
        rows = pl.ds(k * PART, PART)
        arrive(ub.at[near_head, rows], SHARE_CORE + k, core_dev)
        arrive(ub.at[last_head, rows], RELAY + k, core_dev)

        def body(i, carry):
            r = pl.ds(pl.multiple_of(k * PART + i * 16, 16), 16)
            values = [ub[j, r].astype(F32) for j in range(4)]
            total = sum(jnp.sum(v * v, axis=-1, keepdims=True) for v in values)
            scale = lax.rsqrt(total / (4 * SHARE) + EPSILON)
            for j in range(4):
                nb[r, j * SHARE : (j + 1) * SHARE] = (values[j] * scale * gain[j]).astype(BF)
            return carry

        lax.fori_loop(0, PART // 16, body, 0)

    second_step(1, 2, 0)
    natural(1, 1)
    second_step(1, 2, 1)
    natural(1, 2)
    relay(0)
    second_step(1, 3, 0)
    relay(1)
    norm(0)
    second_step(1, 3, 1)
    natural(1, 3)
    norm(1)
    second_step(1, 4, 0)
    second_step(1, 4, 1)
    natural(1, 4)

    order = (0, 2, 1)
    sides = {0: 1, 1: 1, 2: 0}

    def quarters(a):
        return ((a, 1 - a), (1 - a, a), (1 - a, 1 - a))

    for h in order:
        a = sides[h]
        to = lower if a else upper
        lanes = slice(h * GROUP, (h + 1) * GROUP)
        whole = sum(
            jnp.dot(nb[:, j * 1536 : (j + 1) * 1536], w2[j, :, lanes], preferred_element_type=F32)
            for j in range(2)
        )
        for fh in range(2):
            for f in range(2):
                for rh in range(2):
                    at = ((fh * 2 + f) * 2 + rh) * 48
                    pj[h, fh, f, rh] = whole[at : at + 48].astype(BF)
        for i, (fh, rh) in enumerate(quarters(a)):
            send(pj.at[h, fh, :, rh], hq.at[h, i], HALO + h * 3 + i, to[i])

    for h in order:
        a = sides[h]
        source = upper if a else lower

        def place(value, fh, rh):
            for f in range(2):
                at = (fh * 2 + f) * 4 + rh * 2
                x2[h, at : at + 2] = value[f].astype(F32).reshape(2, 24, GROUP)

        place(pj[h, a, :, a], 1 - a, 1 - a)
        for i, (fh, rh) in enumerate(quarters(a)):
            arrive(hq.at[h, i], HALO + h * 3 + i, source[i])
            place(hq[h, i], 1 - fh, 1 - rh)
        for w in range(3):
            def window(part):
                return x2[h, :, w * 8 : w * 8 + 8, part * HDIM : (part + 1) * HDIM].reshape(128, HDIM).astype(BF)

            out = softmax_attend(window(0), window(1), window(2))
            o2[h, :, w * 8 : w * 8 + 8] = out.reshape(16, 8, HDIM)

        def result(fh, f, rh):
            at = (fh * 2 + f) * 4 + rh * 2
            return o2[h, at : at + 2].reshape(48, HDIM).astype(BF)

        lanes = pl.ds(h * HDIM, HDIM)
        for i, (fh, rh) in enumerate(quarters(a)):
            for f in range(2):
                ob[h, fh, f, rh] = result(1 - fh, f, 1 - rh)
            send(ob.at[h, fh, :, rh], lb.at[fh, :, rh, :, lanes], BACK + h * 3 + i, source[i])
        for f in range(2):
            lb[a, f, a, :, lanes] = result(1 - a, f, 1 - a)
    for h in order:
        a = sides[h]
        to = lower if a else upper
        for i, (fh, rh) in enumerate(quarters(a)):
            arrive(lb.at[fh, :, rh, :, pl.ds(h * HDIM, HDIM)], BACK + h * 3 + i, to[i])
    two = pltpu.make_async_copy(lb, two_out, lsem.at[2])
    two.start()
    for copy in sent:
        copy.wait_send()
    upd.wait()
    two.wait()


def shards(stream, qkv1, w_out1, gain, w_qkv2):
    frames, tile_rows, tile_cols, channels = stream.shape
    vmem = pl.BlockSpec(memory_space=pltpu.VMEM)
    anywhere = pl.BlockSpec(memory_space=pl.ANY)
    updated, layer_two = pl.pallas_call(
        kernel,
        name="layers",
        out_shape=(
            jax.ShapeDtypeStruct((TOKENS, SHARE), BF),
            jax.ShapeDtypeStruct((2, 2, 2, 48, GROUP), BF),
        ),
        in_specs=[vmem, vmem, vmem, vmem, anywhere],
        out_specs=(anywhere, anywhere),
        scratch_shapes=[
            pltpu.VMEM((32, WIDE), BF),
            pltpu.VMEM((32, WIDE), BF),
            pltpu.VMEM((4, 32, GROUP), BF),
            pltpu.VMEM((64, 48, GROUP), BF),
            pltpu.VMEM((64, 48, WIDE), BF),
            pltpu.VMEM((2, 1536, GROUP), BF),
            pltpu.VMEM((2, 1536, WIDE), BF),
            pltpu.VMEM((3, 16, 24, GROUP), F32),
            pltpu.VMEM((16, 24, GROUP), F32),
            pltpu.VMEM((2, TOKENS, GROUP), BF),
            pltpu.VMEM((TOKENS, SHARE), BF),
            pltpu.VMEM((TOKENS, SHARE), BF),
            pltpu.VMEM((TOKENS, SHARE), F32),
            pltpu.VMEM((TOKENS, SHARE), BF),
            pltpu.VMEM((4, TOKENS, SHARE), BF),
            pltpu.VMEM((TOKENS, 4 * SHARE), BF),
            pltpu.VMEM((3, 2, 2, 2, 48, GROUP), BF),
            pltpu.VMEM((3, 3, 2, 48, GROUP), BF),
            pltpu.VMEM((3, 16, 24, GROUP), F32),
            pltpu.VMEM((3, 16, 24, HDIM), F32),
            pltpu.VMEM((3, 2, 2, 2, 48, HDIM), BF),
            pltpu.VMEM((2, 2, 2, 48, GROUP), BF),
            pltpu.SemaphoreType.DMA((N_SEM,)),
            pltpu.SemaphoreType.DMA((N_SEM,)),
            pltpu.SemaphoreType.DMA((3,)),
        ],
        compiler_params=pltpu.CompilerParams(
            collective_id=0, has_side_effects=True, vmem_limit_bytes=56 * 2**20
        ),
    )(
        qkv1.transpose(0, 1, 3, 2, 4).reshape(16, 3, 24, GROUP),
        w_out1,
        w_qkv2.transpose(1, 0, 2),
        gain.reshape(4, 1, SHARE),
        stream.reshape(TOKENS, channels),
    )
    return (
        updated.reshape(frames, tile_rows, tile_cols, SHARE),
        layer_two.reshape(frames, tile_rows, tile_cols, GROUP),
    )


def solution(mesh):
    in_specs = (
        P("tm", "row", None, None),
        P("tm", "row", None, None, "head"),
        P(("row", "tm"), "head"),
        P(),
        P(("row", "tm"), None, "head"),
    )
    out_specs = (P("tm", "row", None, "head"), P("tm", "row", None, "head"))
    return jax.shard_map(shards, mesh=mesh, in_specs=in_specs, out_specs=out_specs, check_vma=False)
```

```python
import jax
import jax.numpy as jnp
from jax import lax
from jax.experimental import pallas as pl
from jax.experimental.pallas import tpu as pltpu
from jax.sharding import PartitionSpec as P

MESH = pl.DeviceIdType.MESH
HDIM = 128
EPSILON = 1e-06
TOKENS = 384
SHARE = 768
GROUP = 384
WIDE = 1152
CHUNKS = 2
PART = TOKENS // CHUNKS
BF = jnp.bfloat16
F32 = jnp.float32

OFFSETS = (1, -1, 2, -2, 3, -3, 4)

GROUPS = ((0,), (1, -1), (2, -2), (3, -3), (4,))

FIRST = (0, 8)
SECOND = (16, 32)
PAIR = 96
LINE = 97
LAYER_ONE = 100
CORE_PART = 101
SHARE_X = 102
SHARE_CORE = SHARE_X + CHUNKS
RELAY = SHARE_CORE + CHUNKS
HALO = RELAY + CHUNKS
BACK = HALO + 9
N_SEM = BACK + 9


def softmax_attend(q, k, v):
    scores = lax.dot_general(
        q, k, (((1,), (1,)), ((), ())), preferred_element_type=F32
    ) * HDIM ** (-0.5)
    largest = jnp.max(scores, axis=-1, keepdims=True)
    weights = jnp.exp(scores - largest)
    probabilities = (weights / jnp.sum(weights, axis=-1, keepdims=True)).astype(BF)
    return jnp.dot(probabilities, v, preferred_element_type=F32)


def kernel(
    qkv, wo, wq, gain, stream, upd_out, two_out,
    own, other, line, ga, gb, w1, w2, x1, l1f, l1, ps, pr, xf, st, ub, nb, pj, hq, x2, o2, ob, lb,
    ssem, rsem, lsem,
):
    row = lax.axis_index("row")
    z = lax.axis_index("tm")
    head = lax.axis_index("head")
    xl, y = row // 8, row % 8
    xh, c = head // 2, head % 2

    def first(d):
        return (xl * 8 + (y + c * (d + 8)) % 8, (z + (1 - c) * (d + 8)) % 8, head)

    def second(d):
        return (xl * 8 + (y + (1 - c) * (d + 8)) % 8, (z + c * (d + 8)) % 8, head)

    p0 = (1 - c) * z + c * y
    s0 = (1 - c) * y + c * z
    pair_dev = ((row + 8) % 16, z, head)
    core_dev = (row, z, xh * 2 + (1 - c))
    x_dev = (row, z, (head + 2) % 4)
    cross_dev = ((row + 8) % 16, z, (head + 2) % 4)
    row_m, row_p = (row + 15) % 16, (row + 1) % 16
    z_m, z_p = (z + 7) % 8, (z + 1) % 8
    lower = ((row_m, z, head), (row, z_m, head), (row_m, z_m, head))
    upper = ((row_p, z, head), (row, z_p, head), (row_p, z_p, head))

    barrier = pltpu.get_barrier_semaphore()
    greet = (second(1), second(-1), pair_dev, core_dev, x_dev, cross_dev) + lower + upper
    greet += tuple(first(d) for d in OFFSETS)
    for device in greet:
        pl.semaphore_signal(barrier, inc=1, device_id=device, device_id_type=MESH)
    pl.semaphore_wait(barrier, len(greet))

    sent = []

    def send(src, dst, k, device):
        copy = pltpu.make_async_remote_copy(
            src_ref=src, dst_ref=dst, send_sem=ssem.at[k], recv_sem=rsem.at[k],
            device_id=device, device_id_type=MESH,
        )
        copy.start()
        sent.append(copy)

    def arrive(dst, k, device):
        pltpu.make_async_remote_copy(
            src_ref=dst, dst_ref=dst, send_sem=ssem.at[k], recv_sem=rsem.at[k],
            device_id=device, device_id_type=MESH,
        ).wait_recv()

    at_x = xh * 2 + xl
    tail = jnp.zeros((8, GROUP), F32)
    line[at_x] = jnp.concatenate([wo[...].astype(F32), tail], axis=0).astype(BF)
    for i, device in enumerate((pair_dev, x_dev, cross_dev)):
        send(line.at[at_x], line.at[at_x], LINE + i, device)
    mine = jnp.concatenate(
        [wq[part, :, h * HDIM : (h + 1) * HDIM].astype(F32) for h in range(3) for part in range(3)], axis=1
    )
    own[...] = jnp.concatenate([mine, jnp.zeros((8, WIDE), F32)], axis=0).astype(BF)
    send(own, other, PAIR, pair_dev)

    stream_in = pltpu.make_async_copy(
        stream.at[:, pl.ds(pl.multiple_of(head * SHARE, SHARE), SHARE)], st, lsem.at[0]
    )
    stream_in.start()

    def widen(i, carry):
        for part in range(3):
            x1[part, i] = qkv[i, part].astype(F32)
        return carry

    def attend_one(w):
        def unit(h, carry):
            lanes = pl.ds(pl.multiple_of(h * HDIM, HDIM), HDIM)

            def window(part):
                return x1[part, :, w * 8 : w * 8 + 8, lanes].reshape(128, HDIM).astype(BF)

            out = softmax_attend(window(0), window(1), window(2))
            l1f[:, w * 8 : w * 8 + 8, lanes] = out.reshape(16, 8, HDIM)
            return carry

        lax.fori_loop(0, 3, unit, 0)

    def at_line(flip_low, flip_high):
        return (xh + flip_high * (1 - 2 * xh)) * 2 + xl + flip_low * (1 - 2 * xl)

    arrive(line.at[at_line(1, 0)], LINE, pair_dev)
    arrive(line.at[at_line(0, 1)], LINE + 1, x_dev)
    arrive(line.at[at_line(1, 1)], LINE + 2, cross_dev)
    here = s0 * 8 + p0
    ga[here] = jnp.concatenate(
        [line[xh].astype(F32)[:24], line[2 + xh].astype(F32)[:24]], axis=0
    ).astype(BF)
    bufs = (ga, gb)

    def spread():
        for i, d in enumerate(OFFSETS):
            send(ga.at[here], ga.at[here], FIRST[0] + i, first(d))

    def spread_arrive():
        for i, d in enumerate(OFFSETS):
            arrive(ga.at[s0 * 8 + (p0 - d + 8) % 8], FIRST[0] + i, first(-d))

    def first_send(d, hop):
        slot = gb.at[s0 * 8 + (p0 + (1 - 2 * d) * (1 - hop) + 8) % 8]
        send(slot, slot, FIRST[1] + d * 4 + hop - 1, first(1 - 2 * d))

    def first_step(hop):
        for d in range(2):
            if hop == 4 and d == 0:
                continue
            slot = gb.at[s0 * 8 + (p0 - (1 - 2 * d) * hop + 8) % 8]
            arrive(slot, FIRST[1] + d * 4 + hop - 1, first(2 * d - 1))
            if hop < 3 or (hop == 3 and d == 1):
                first_send(d, hop + 1)

    def slab_slot(s, q):
        return ga.at[pl.ds(pl.multiple_of(s * 8 + q * 4, 4), 4)]

    def slab_send(d, hop, q):
        slot = slab_slot((s0 + (1 - 2 * d) * (1 - hop) + 8) % 8, q)
        send(slot, slot, SECOND[0] + d * 8 + (hop - 1) * 2 + q, second(1 - 2 * d))

    def slab_start():
        for q in range(2):
            for d in range(2):
                slab_send(d, 1, q)

    def slab_step(hop):
        for q in range(2):
            for d in range(2):
                if hop == 4 and d != q:
                    continue
                slot = slab_slot((s0 - (1 - 2 * d) * hop + 8) % 8, q)
                arrive(slot, SECOND[0] + d * 8 + (hop - 1) * 2 + q, second(2 * d - 1))
                if hop < 3 or (hop == 3 and d == q):
                    slab_send(d, hop + 1, q)

    def shard_slot(s, o):
        return gb.at[s * 8 + (p0 + o + 8) % 8]

    def shard_number(d, hop, o):
        return SECOND[1] + (hop - 1) * 16 + (o % 8) * 2 + d

    def shard_send(d, hop, o):
        slot = shard_slot((s0 + (1 - 2 * d) * (1 - hop) + 8) % 8, o)
        send(slot, slot, shard_number(d, hop, o), second(1 - 2 * d))

    def shard_start(g):
        for o in GROUPS[g]:
            for d in range(2):
                shard_send(d, 1, o)

    def shard_step(hop, *groups):
        for g in groups:
            for o in GROUPS[g]:
                for d in range(2):
                    last = d == (0 if o > 0 else 1)
                    if hop == 4 and not last:
                        continue
                    slot = shard_slot((s0 - (1 - 2 * d) * hop + 8) % 8, o)
                    arrive(slot, shard_number(d, hop, o), second(2 * d - 1))
                    if hop < 3 or (hop == 3 and last):
                        shard_send(d, hop + 1, o)

    outs = (w1, w2)
    m0, odd = s0 // 2, s0 % 2
    ready = (m0, (m0 + 3 + 2 * odd) % 4, (m0 + 1 + 2 * odd) % 4, (m0 + 2) % 4)

    def natural(a, hop):
        m = ready[hop - 1]
        src, dst = bufs[a], outs[a]

        def body(i, carry):
            one = 16 * m + (1 - c) * 2 * i + c * i
            two = one + 1 + 7 * c
            at = (1 - c) * (8 * m + i) + c * (4 * i + m)
            g0, g1 = src[one].astype(F32), src[two].astype(F32)
            rows = pl.ds(pl.multiple_of(at * 48, 48), 48)
            dst[0, rows] = jnp.concatenate([g0[:24], g1[:24]], axis=0).astype(BF)
            dst[1, rows] = jnp.concatenate([g0[24:], g1[24:]], axis=0).astype(BF)
            return carry

        lax.fori_loop(0, 8, body, 0)

    spread()
    arrive(other, PAIR, pair_dev)
    theirs = other[...].astype(F32)[:24]
    gb[here] = jnp.concatenate(
        [jnp.where(xl == 0, mine, theirs), jnp.where(xl == 0, theirs, mine)], axis=0
    ).astype(BF)
    for d in range(2):
        first_send(d, 1)
    shard_start(0)
    lax.fori_loop(0, 16, widen, 0)
    attend_one(0)
    first_step(1)
    shard_start(1)
    spread_arrive()
    slab_start()
    first_step(2)
    shard_start(2)
    attend_one(1)
    first_step(3)
    shard_start(3)
    slab_step(1)
    first_step(4)
    shard_start(4)
    shard_step(1, 0)
    attend_one(2)
    l1[xh] = l1f[...].reshape(TOKENS, GROUP).astype(BF)
    send(l1.at[xh], l1.at[xh], LAYER_ONE, x_dev)
    slab_step(2)
    natural(0, 1)
    shard_step(1, 1, 2)
    slab_step(3)
    natural(0, 2)
    shard_step(1, 3)
    natural(0, 3)
    slab_step(4)
    natural(0, 4)

    arrive(l1.at[1 - xh], LAYER_ONE, x_dev)

    def partial(share, n):
        rows = pl.ds(pl.multiple_of(share * SHARE + n * 256, 256), 256)
        return sum(
            lax.dot_general(
                l1[j], w1[j, rows], (((1,), (1,)), ((), ())), preferred_element_type=F32
            )
            for j in range(2)
        )

    for n in range(3):
        ps[:, n * 256 : (n + 1) * 256] = partial(1 - c, n).astype(BF)
    send(ps, pr, CORE_PART, core_dev)
    stream_in.wait()
    for n in range(3):
        cols = slice(n * 256, (n + 1) * 256)
        xf[:, cols] = partial(c, n) + st[:, cols].astype(F32)
    arrive(pr, CORE_PART, core_dev)
    for k in range(CHUNKS):
        rows = pl.ds(k * PART, PART)
        ub[head, rows] = (xf[rows] + pr[rows].astype(F32)).astype(BF)
        send(ub.at[head, rows], ub.at[head, rows], SHARE_X + k, x_dev)
        send(ub.at[head, rows], ub.at[head, rows], SHARE_CORE + k, core_dev)
    upd = pltpu.make_async_copy(ub.at[head], upd_out, lsem.at[1])
    upd.start()

    far_head = (head + 2) % 4
    near_head = xh * 2 + 1 - c
    last_head = (near_head + 2) % 4

    def relay(k):
        rows = pl.ds(k * PART, PART)
        arrive(ub.at[far_head, rows], SHARE_X + k, x_dev)
        send(ub.at[far_head, rows], ub.at[far_head, rows], RELAY + k, core_dev)

    def norm(k):
        rows = pl.ds(k * PART, PART)
        arrive(ub.at[near_head, rows], SHARE_CORE + k, core_dev)
        arrive(ub.at[last_head, rows], RELAY + k, core_dev)

        def body(i, carry):
            r = pl.ds(pl.multiple_of(k * PART + i * 16, 16), 16)
            values = [ub[j, r].astype(F32) for j in range(4)]
            total = sum(jnp.sum(v * v, axis=-1, keepdims=True) for v in values)
            scale = lax.rsqrt(total / (4 * SHARE) + EPSILON)
            for j in range(4):
                nb[r, j * SHARE : (j + 1) * SHARE] = (values[j] * scale * gain[j]).astype(BF)
            return carry

        lax.fori_loop(0, PART // 16, body, 0)

    shard_step(1, 4)
    shard_step(2, 0, 1)
    natural(1, 1)
    shard_step(2, 2, 3, 4)
    relay(0)
    natural(1, 2)
    shard_step(3, 0, 1)
    relay(1)
    norm(0)
    shard_step(3, 2, 3)
    norm(1)
    shard_step(3, 4)
    natural(1, 3)
    shard_step(4, 0, 1, 2, 3, 4)
    natural(1, 4)

    order = (0, 2, 1)
    sides = {0: 1, 1: 1, 2: 0}

    def quarters(a):
        return ((a, 1 - a), (1 - a, a), (1 - a, 1 - a))

    for h in order:
        a = sides[h]
        to = lower if a else upper
        lanes = slice(h * GROUP, (h + 1) * GROUP)
        whole = sum(
            jnp.dot(nb[:, j * 1536 : (j + 1) * 1536], w2[j, :, lanes], preferred_element_type=F32)
            for j in range(2)
        )
        for fh in range(2):
            for f in range(2):
                for rh in range(2):
                    at = ((fh * 2 + f) * 2 + rh) * 48
                    pj[h, fh, f, rh] = whole[at : at + 48].astype(BF)
        for i, (fh, rh) in enumerate(quarters(a)):
            send(pj.at[h, fh, :, rh], hq.at[h, i], HALO + h * 3 + i, to[i])

    for h in order:
        a = sides[h]
        source = upper if a else lower

        def place(value, fh, rh):
            for f in range(2):
                at = (fh * 2 + f) * 4 + rh * 2
                x2[h, at : at + 2] = value[f].astype(F32).reshape(2, 24, GROUP)

        place(pj[h, a, :, a], 1 - a, 1 - a)
        for i, (fh, rh) in enumerate(quarters(a)):
            arrive(hq.at[h, i], HALO + h * 3 + i, source[i])
            place(hq[h, i], 1 - fh, 1 - rh)
        for w in range(3):
            def window(part):
                return x2[h, :, w * 8 : w * 8 + 8, part * HDIM : (part + 1) * HDIM].reshape(128, HDIM).astype(BF)

            out = softmax_attend(window(0), window(1), window(2))
            o2[h, :, w * 8 : w * 8 + 8] = out.reshape(16, 8, HDIM)

        def result(fh, f, rh):
            at = (fh * 2 + f) * 4 + rh * 2
            return o2[h, at : at + 2].reshape(48, HDIM).astype(BF)

        lanes = pl.ds(h * HDIM, HDIM)
        for i, (fh, rh) in enumerate(quarters(a)):
            for f in range(2):
                ob[h, fh, f, rh] = result(1 - fh, f, 1 - rh)
            send(ob.at[h, fh, :, rh], lb.at[fh, :, rh, :, lanes], BACK + h * 3 + i, source[i])
        for f in range(2):
            lb[a, f, a, :, lanes] = result(1 - a, f, 1 - a)
    for h in order:
        a = sides[h]
        to = lower if a else upper
        for i, (fh, rh) in enumerate(quarters(a)):
            arrive(lb.at[fh, :, rh, :, pl.ds(h * HDIM, HDIM)], BACK + h * 3 + i, to[i])
    two = pltpu.make_async_copy(lb, two_out, lsem.at[2])
    two.start()
    for copy in sent:
        copy.wait_send()
    upd.wait()
    two.wait()


def hand_over(one, two, one_out, two_out):
    one_out[...] = one[...]
    two_out[...] = two[...]


def shards(stream, qkv1, w_out1, gain, w_qkv2):
    frames, tile_rows, tile_cols, channels = stream.shape
    vmem = pl.BlockSpec(memory_space=pltpu.VMEM)
    anywhere = pl.BlockSpec(memory_space=pl.ANY)
    updated, layer_two = pl.pallas_call(
        kernel,
        name="layers",
        out_shape=(
            jax.ShapeDtypeStruct((TOKENS, SHARE), BF),
            jax.ShapeDtypeStruct((2, 2, 2, 48, GROUP), BF),
        ),
        in_specs=[vmem, vmem, vmem, vmem, anywhere],
        out_specs=(anywhere, anywhere),
        scratch_shapes=[
            pltpu.VMEM((32, WIDE), BF),
            pltpu.VMEM((32, WIDE), BF),
            pltpu.VMEM((4, 32, GROUP), BF),
            pltpu.VMEM((64, 48, GROUP), BF),
            pltpu.VMEM((64, 48, WIDE), BF),
            pltpu.VMEM((2, 1536, GROUP), BF),
            pltpu.VMEM((2, 1536, WIDE), BF),
            pltpu.VMEM((3, 16, 24, GROUP), F32),
            pltpu.VMEM((16, 24, GROUP), F32),
            pltpu.VMEM((2, TOKENS, GROUP), BF),
            pltpu.VMEM((TOKENS, SHARE), BF),
            pltpu.VMEM((TOKENS, SHARE), BF),
            pltpu.VMEM((TOKENS, SHARE), F32),
            pltpu.VMEM((TOKENS, SHARE), BF),
            pltpu.VMEM((4, TOKENS, SHARE), BF),
            pltpu.VMEM((TOKENS, 4 * SHARE), BF),
            pltpu.VMEM((3, 2, 2, 2, 48, GROUP), BF),
            pltpu.VMEM((3, 3, 2, 48, GROUP), BF),
            pltpu.VMEM((3, 16, 24, GROUP), F32),
            pltpu.VMEM((3, 16, 24, HDIM), F32),
            pltpu.VMEM((3, 2, 2, 2, 48, HDIM), BF),
            pltpu.VMEM((2, 2, 2, 48, GROUP), BF),
            pltpu.SemaphoreType.DMA((N_SEM,)),
            pltpu.SemaphoreType.DMA((N_SEM,)),
            pltpu.SemaphoreType.DMA((3,)),
        ],
        compiler_params=pltpu.CompilerParams(
            collective_id=0, has_side_effects=True, vmem_limit_bytes=56 * 2**20
        ),
    )(
        qkv1.transpose(0, 1, 3, 2, 4).reshape(16, 3, 24, GROUP),
        w_out1,
        w_qkv2.transpose(1, 0, 2),
        gain.reshape(4, 1, SHARE),
        stream.reshape(TOKENS, channels),
    )
    updated, layer_two = pl.pallas_call(
        hand_over,
        name="outputs",
        out_shape=(
            jax.ShapeDtypeStruct((TOKENS, SHARE), BF),
            jax.ShapeDtypeStruct((TOKENS, GROUP), BF),
        ),
        in_specs=[vmem, vmem],
        out_specs=(vmem, vmem),
    )(updated, layer_two.reshape(TOKENS, GROUP))
    return (
        updated.reshape(frames, tile_rows, tile_cols, SHARE),
        layer_two.reshape(frames, tile_rows, tile_cols, GROUP),
    )


def solution(mesh):
    in_specs = (
        P("tm", "row", None, None),
        P("tm", "row", None, None, "head"),
        P(("row", "tm"), "head"),
        P(),
        P(("row", "tm"), None, "head"),
    )
    out_specs = (P("tm", "row", None, "head"), P("tm", "row", None, "head"))
    return jax.shard_map(shards, mesh=mesh, in_specs=in_specs, out_specs=out_specs, check_vma=False)
```

```python
import jax
import jax.numpy as jnp
from jax import lax
from jax.experimental import pallas as pl
from jax.experimental.pallas import tpu as pltpu
from jax.sharding import PartitionSpec as P

MESH = pl.DeviceIdType.MESH
HDIM = 128
EPSILON = 1e-06
TOKENS = 384
SHARE = 768
GROUP = 384
WIDE = 1152
CHUNKS = 4
PART = TOKENS // CHUNKS
BF = jnp.bfloat16
F32 = jnp.float32

OFFSETS = (1, -1, 2, -2, 3, -3, 4)

GROUPS = ((0,), (1, -1), (2, -2), (3, -3), (4,))

FIRST = (0, 8)
SECOND = (16, 32)
PAIR = 96
LINE = 97
LAYER_ONE = 100
CORE_PART = 101
SHARE_X = 102
SHARE_CORE = SHARE_X + CHUNKS
RELAY = SHARE_CORE + CHUNKS
HALO = RELAY + CHUNKS
BACK = HALO + 9
N_SEM = BACK + 9


def softmax_attend(q, k, v):
    scores = lax.dot_general(
        q, k, (((1,), (1,)), ((), ())), preferred_element_type=F32
    ) * HDIM ** (-0.5)
    largest = jnp.max(scores, axis=-1, keepdims=True)
    weights = jnp.exp(scores - largest)
    probabilities = (weights / jnp.sum(weights, axis=-1, keepdims=True)).astype(BF)
    return jnp.dot(probabilities, v, preferred_element_type=F32)


def kernel(
    qkv, wo, wq, gain, stream, upd_out, two_out,
    own, other, line, ga, gb, w1, w2, x1, l1f, l1, ps, pr, xf, st, ub, nb, pj, hq, x2, o2, ob, lb, lr,
    ssem, rsem, lsem,
):
    row = lax.axis_index("row")
    z = lax.axis_index("tm")
    head = lax.axis_index("head")
    xl, y = row // 8, row % 8
    xh, c = head // 2, head % 2

    def first(d):
        return (xl * 8 + (y + c * (d + 8)) % 8, (z + (1 - c) * (d + 8)) % 8, head)

    def second(d):
        return (xl * 8 + (y + (1 - c) * (d + 8)) % 8, (z + c * (d + 8)) % 8, head)

    p0 = (1 - c) * z + c * y
    s0 = (1 - c) * y + c * z
    pair_dev = ((row + 8) % 16, z, head)
    core_dev = (row, z, xh * 2 + (1 - c))
    x_dev = (row, z, (head + 2) % 4)
    cross_dev = ((row + 8) % 16, z, (head + 2) % 4)
    row_m, row_p = (row + 15) % 16, (row + 1) % 16
    z_m, z_p = (z + 7) % 8, (z + 1) % 8
    lower = ((row_m, z, head), (row, z_m, head), (row_m, z_m, head))
    upper = ((row_p, z, head), (row, z_p, head), (row_p, z_p, head))

    barrier = pltpu.get_barrier_semaphore()
    greet = (second(1), second(-1), pair_dev, core_dev, x_dev, cross_dev) + lower + upper
    greet += tuple(first(d) for d in OFFSETS)
    for device in greet:
        pl.semaphore_signal(barrier, inc=1, device_id=device, device_id_type=MESH)
    pl.semaphore_wait(barrier, len(greet))

    sent = []

    def send(src, dst, k, device):
        copy = pltpu.make_async_remote_copy(
            src_ref=src, dst_ref=dst, send_sem=ssem.at[k], recv_sem=rsem.at[k],
            device_id=device, device_id_type=MESH,
        )
        copy.start()
        sent.append(copy)

    def arrive(dst, k, device):
        pltpu.make_async_remote_copy(
            src_ref=dst, dst_ref=dst, send_sem=ssem.at[k], recv_sem=rsem.at[k],
            device_id=device, device_id_type=MESH,
        ).wait_recv()

    at_x = xh * 2 + xl
    tail = jnp.zeros((8, GROUP), F32)
    line[at_x] = jnp.concatenate([wo[...].astype(F32), tail], axis=0).astype(BF)
    for i, device in enumerate((pair_dev, x_dev, cross_dev)):
        send(line.at[at_x], line.at[at_x], LINE + i, device)
    mine = jnp.concatenate(
        [wq[part, :, h * HDIM : (h + 1) * HDIM].astype(F32) for h in range(3) for part in range(3)], axis=1
    )
    own[...] = jnp.concatenate([mine, jnp.zeros((8, WIDE), F32)], axis=0).astype(BF)
    send(own, other, PAIR, pair_dev)

    stream_in = pltpu.make_async_copy(
        stream.at[:, pl.ds(pl.multiple_of(head * SHARE, SHARE), SHARE)], st, lsem.at[0]
    )
    stream_in.start()

    def widen(i, carry):
        for part in range(3):
            x1[part, i] = qkv[i, part].astype(F32)
        return carry

    def attend_one(w):
        def unit(h, carry):
            lanes = pl.ds(pl.multiple_of(h * HDIM, HDIM), HDIM)

            def window(part):
                return x1[part, :, w * 8 : w * 8 + 8, lanes].reshape(128, HDIM).astype(BF)

            out = softmax_attend(window(0), window(1), window(2))
            l1f[:, w * 8 : w * 8 + 8, lanes] = out.reshape(16, 8, HDIM)
            return carry

        lax.fori_loop(0, 3, unit, 0)

    def at_line(flip_low, flip_high):
        return (xh + flip_high * (1 - 2 * xh)) * 2 + xl + flip_low * (1 - 2 * xl)

    arrive(line.at[at_line(1, 0)], LINE, pair_dev)
    arrive(line.at[at_line(0, 1)], LINE + 1, x_dev)
    arrive(line.at[at_line(1, 1)], LINE + 2, cross_dev)
    here = s0 * 8 + p0
    ga[here] = jnp.concatenate(
        [line[xh].astype(F32)[:24], line[2 + xh].astype(F32)[:24]], axis=0
    ).astype(BF)
    bufs = (ga, gb)

    def spread():
        for i, d in enumerate(OFFSETS):
            send(ga.at[here], ga.at[here], FIRST[0] + i, first(d))

    def spread_arrive():
        for i, d in enumerate(OFFSETS):
            arrive(ga.at[s0 * 8 + (p0 - d + 8) % 8], FIRST[0] + i, first(-d))

    def first_send(d, hop):
        slot = gb.at[s0 * 8 + (p0 + (1 - 2 * d) * (1 - hop) + 8) % 8]
        send(slot, slot, FIRST[1] + d * 4 + hop - 1, first(1 - 2 * d))

    def first_step(hop):
        for d in range(2):
            if hop == 4 and d == 0:
                continue
            slot = gb.at[s0 * 8 + (p0 - (1 - 2 * d) * hop + 8) % 8]
            arrive(slot, FIRST[1] + d * 4 + hop - 1, first(2 * d - 1))
            if hop < 3 or (hop == 3 and d == 1):
                first_send(d, hop + 1)

    def slab_slot(s, q):
        return ga.at[pl.ds(pl.multiple_of(s * 8 + q * 4, 4), 4)]

    def slab_send(d, hop, q):
        slot = slab_slot((s0 + (1 - 2 * d) * (1 - hop) + 8) % 8, q)
        send(slot, slot, SECOND[0] + d * 8 + (hop - 1) * 2 + q, second(1 - 2 * d))

    def slab_start():
        for q in range(2):
            for d in range(2):
                slab_send(d, 1, q)

    def slab_step(hop):
        for q in range(2):
            for d in range(2):
                if hop == 4 and d != q:
                    continue
                slot = slab_slot((s0 - (1 - 2 * d) * hop + 8) % 8, q)
                arrive(slot, SECOND[0] + d * 8 + (hop - 1) * 2 + q, second(2 * d - 1))
                if hop < 3 or (hop == 3 and d == q):
                    slab_send(d, hop + 1, q)

    def shard_slot(s, o):
        return gb.at[s * 8 + (p0 + o + 8) % 8]

    def shard_number(d, hop, o):
        return SECOND[1] + (hop - 1) * 16 + (o % 8) * 2 + d

    def shard_send(d, hop, o):
        slot = shard_slot((s0 + (1 - 2 * d) * (1 - hop) + 8) % 8, o)
        send(slot, slot, shard_number(d, hop, o), second(1 - 2 * d))

    def shard_start(g):
        for o in GROUPS[g]:
            for d in range(2):
                shard_send(d, 1, o)

    def shard_step(hop, *groups):
        for g in groups:
            for o in GROUPS[g]:
                for d in range(2):
                    last = d == (0 if o > 0 else 1)
                    if hop == 4 and not last:
                        continue
                    slot = shard_slot((s0 - (1 - 2 * d) * hop + 8) % 8, o)
                    arrive(slot, shard_number(d, hop, o), second(2 * d - 1))
                    if hop < 3 or (hop == 3 and last):
                        shard_send(d, hop + 1, o)

    outs = (w1, w2)
    m0, odd = s0 // 2, s0 % 2
    ready = (m0, (m0 + 3 + 2 * odd) % 4, (m0 + 1 + 2 * odd) % 4, (m0 + 2) % 4)

    def natural(a, hop):
        m = ready[hop - 1]
        src, dst = bufs[a], outs[a]

        def body(i, carry):
            one = 16 * m + (1 - c) * 2 * i + c * i
            two = one + 1 + 7 * c
            at = (1 - c) * (8 * m + i) + c * (4 * i + m)
            g0, g1 = src[one].astype(F32), src[two].astype(F32)
            rows = pl.ds(pl.multiple_of(at * 48, 48), 48)
            dst[0, rows] = jnp.concatenate([g0[:24], g1[:24]], axis=0).astype(BF)
            dst[1, rows] = jnp.concatenate([g0[24:], g1[24:]], axis=0).astype(BF)
            return carry

        lax.fori_loop(0, 8, body, 0)

    spread()
    arrive(other, PAIR, pair_dev)
    theirs = other[...].astype(F32)[:24]
    gb[here] = jnp.concatenate(
        [jnp.where(xl == 0, mine, theirs), jnp.where(xl == 0, theirs, mine)], axis=0
    ).astype(BF)
    for d in range(2):
        first_send(d, 1)
    shard_start(0)
    lax.fori_loop(0, 16, widen, 0)
    attend_one(0)
    first_step(1)
    shard_start(1)
    spread_arrive()
    slab_start()
    first_step(2)
    shard_start(2)
    attend_one(1)
    first_step(3)
    slab_step(1)
    shard_start(3)
    first_step(4)
    shard_step(1, 0)
    attend_one(2)
    l1[xh] = l1f[...].reshape(TOKENS, GROUP).astype(BF)
    send(l1.at[xh], l1.at[xh], LAYER_ONE, x_dev)
    slab_step(2)
    shard_start(4)
    natural(0, 1)
    shard_step(1, 1, 2)
    slab_step(3)
    natural(0, 2)
    shard_step(1, 3)
    natural(0, 3)
    slab_step(4)
    natural(0, 4)

    arrive(l1.at[1 - xh], LAYER_ONE, x_dev)

    def partial(share, n):
        rows = pl.ds(pl.multiple_of(share * SHARE + n * 256, 256), 256)
        return sum(
            lax.dot_general(
                l1[j], w1[j, rows], (((1,), (1,)), ((), ())), preferred_element_type=F32
            )
            for j in range(2)
        )

    for n in range(3):
        ps[:, n * 256 : (n + 1) * 256] = partial(1 - c, n).astype(BF)
    send(ps, pr, CORE_PART, core_dev)
    stream_in.wait()
    for n in range(3):
        cols = slice(n * 256, (n + 1) * 256)
        xf[:, cols] = partial(c, n) + st[:, cols].astype(F32)
    arrive(pr, CORE_PART, core_dev)
    for k in range(CHUNKS):
        rows = pl.ds(k * PART, PART)
        ub[head, rows] = (xf[rows] + pr[rows].astype(F32)).astype(BF)
        send(ub.at[head, rows], ub.at[head, rows], SHARE_X + k, x_dev)
        send(ub.at[head, rows], ub.at[head, rows], SHARE_CORE + k, core_dev)
    upd = pltpu.make_async_copy(ub.at[head], upd_out, lsem.at[1])
    upd.start()

    far_head = (head + 2) % 4
    near_head = xh * 2 + 1 - c
    last_head = (near_head + 2) % 4

    def relay(k):
        rows = pl.ds(k * PART, PART)
        arrive(ub.at[far_head, rows], SHARE_X + k, x_dev)
        send(ub.at[far_head, rows], ub.at[far_head, rows], RELAY + k, core_dev)

    def norm(k):
        rows = pl.ds(k * PART, PART)
        arrive(ub.at[near_head, rows], SHARE_CORE + k, core_dev)
        arrive(ub.at[last_head, rows], RELAY + k, core_dev)

        def body(i, carry):
            r = pl.ds(pl.multiple_of(k * PART + i * 16, 16), 16)
            values = [ub[j, r].astype(F32) for j in range(4)]
            total = sum(jnp.sum(v * v, axis=-1, keepdims=True) for v in values)
            scale = lax.rsqrt(total / (4 * SHARE) + EPSILON)
            for j in range(4):
                nb[r, j * SHARE : (j + 1) * SHARE] = (values[j] * scale * gain[j]).astype(BF)
            return carry

        lax.fori_loop(0, PART // 16, body, 0)

    shard_step(1, 4)
    shard_step(2, 0, 1)
    natural(1, 1)
    shard_step(2, 2, 3, 4)
    relay(0)
    relay(1)
    natural(1, 2)
    shard_step(3, 0, 1)
    relay(2)
    relay(3)
    norm(0)
    norm(1)
    shard_step(3, 2, 3)
    norm(2)
    shard_step(3, 4)
    norm(3)
    natural(1, 3)
    shard_step(4, 0, 1, 2, 3, 4)
    natural(1, 4)

    order = (0, 2, 1)
    sides = {0: 1, 1: 1, 2: 0}

    def quarters(a):
        return ((a, 1 - a), (1 - a, a), (1 - a, 1 - a))

    for h in order:
        a = sides[h]
        to = lower if a else upper
        lanes = slice(h * GROUP, (h + 1) * GROUP)
        whole = sum(
            jnp.dot(nb[:, j * 1536 : (j + 1) * 1536], w2[j, :, lanes], preferred_element_type=F32)
            for j in range(2)
        )
        for fh in range(2):
            for f in range(2):
                for rh in range(2):
                    at = ((fh * 2 + f) * 2 + rh) * 48
                    pj[h, fh, f, rh] = whole[at : at + 48].astype(BF)
        for i, (fh, rh) in enumerate(quarters(a)):
            send(pj.at[h, fh, :, rh], hq.at[h, i], HALO + h * 3 + i, to[i])

    for h in order:
        a = sides[h]
        source = upper if a else lower

        def place(value, fh, rh):
            for f in range(2):
                at = (fh * 2 + f) * 4 + rh * 2
                x2[h, at : at + 2] = value[f].astype(F32).reshape(2, 24, GROUP)

        place(pj[h, a, :, a], 1 - a, 1 - a)
        for i, (fh, rh) in enumerate(quarters(a)):
            arrive(hq.at[h, i], HALO + h * 3 + i, source[i])
            place(hq[h, i], 1 - fh, 1 - rh)
        for w in range(3):
            def window(part):
                return x2[h, :, w * 8 : w * 8 + 8, part * HDIM : (part + 1) * HDIM].reshape(128, HDIM).astype(BF)

            out = softmax_attend(window(0), window(1), window(2))
            o2[h, :, w * 8 : w * 8 + 8] = out.reshape(16, 8, HDIM)

        def result(fh, f, rh):
            at = (fh * 2 + f) * 4 + rh * 2
            return o2[h, at : at + 2].reshape(48, HDIM).astype(BF)

        for i, (fh, rh) in enumerate(quarters(a)):
            for f in range(2):
                ob[h, fh, f, rh] = result(1 - fh, f, 1 - rh)
            send(ob.at[h, fh, :, rh], lb.at[h, fh, :, rh], BACK + h * 3 + i, source[i])
        for f in range(2):
            lb[h, a, f, a] = result(1 - a, f, 1 - a)
    for h in order:
        a = sides[h]
        to = lower if a else upper
        for i, (fh, rh) in enumerate(quarters(a)):
            arrive(lb.at[h, fh, :, rh], BACK + h * 3 + i, to[i])
        lr[:, h * HDIM : (h + 1) * HDIM] = lb[h].reshape(TOKENS, HDIM)
    two = pltpu.make_async_copy(lr, two_out, lsem.at[2])
    two.start()
    for copy in sent:
        copy.wait_send()
    upd.wait()
    two.wait()


def hand_over(one, two, one_out, two_out):
    one_out[...] = one[...]
    two_out[...] = two[...]


def shards(stream, qkv1, w_out1, gain, w_qkv2):
    frames, tile_rows, tile_cols, channels = stream.shape
    vmem = pl.BlockSpec(memory_space=pltpu.VMEM)
    anywhere = pl.BlockSpec(memory_space=pl.ANY)
    updated, layer_two = pl.pallas_call(
        kernel,
        name="layers",
        out_shape=(
            jax.ShapeDtypeStruct((TOKENS, SHARE), BF),
            jax.ShapeDtypeStruct((TOKENS, GROUP), BF),
        ),
        in_specs=[vmem, vmem, vmem, vmem, anywhere],
        out_specs=(anywhere, anywhere),
        scratch_shapes=[
            pltpu.VMEM((32, WIDE), BF),
            pltpu.VMEM((32, WIDE), BF),
            pltpu.VMEM((4, 32, GROUP), BF),
            pltpu.VMEM((64, 48, GROUP), BF),
            pltpu.VMEM((64, 48, WIDE), BF),
            pltpu.VMEM((2, 1536, GROUP), BF),
            pltpu.VMEM((2, 1536, WIDE), BF),
            pltpu.VMEM((3, 16, 24, GROUP), F32),
            pltpu.VMEM((16, 24, GROUP), F32),
            pltpu.VMEM((2, TOKENS, GROUP), BF),
            pltpu.VMEM((TOKENS, SHARE), BF),
            pltpu.VMEM((TOKENS, SHARE), BF),
            pltpu.VMEM((TOKENS, SHARE), F32),
            pltpu.VMEM((TOKENS, SHARE), BF),
            pltpu.VMEM((4, TOKENS, SHARE), BF),
            pltpu.VMEM((TOKENS, 4 * SHARE), BF),
            pltpu.VMEM((3, 2, 2, 2, 48, GROUP), BF),
            pltpu.VMEM((3, 3, 2, 48, GROUP), BF),
            pltpu.VMEM((3, 16, 24, GROUP), F32),
            pltpu.VMEM((3, 16, 24, HDIM), F32),
            pltpu.VMEM((3, 2, 2, 2, 48, HDIM), BF),
            pltpu.VMEM((3, 2, 2, 2, 48, HDIM), BF),
            pltpu.VMEM((TOKENS, GROUP), BF),
            pltpu.SemaphoreType.DMA((N_SEM,)),
            pltpu.SemaphoreType.DMA((N_SEM,)),
            pltpu.SemaphoreType.DMA((3,)),
        ],
        compiler_params=pltpu.CompilerParams(
            collective_id=0, has_side_effects=True, vmem_limit_bytes=56 * 2**20
        ),
    )(
        qkv1.transpose(0, 1, 3, 2, 4).reshape(16, 3, 24, GROUP),
        w_out1,
        w_qkv2.transpose(1, 0, 2),
        gain.reshape(4, 1, SHARE),
        stream.reshape(TOKENS, channels),
    )
    updated, layer_two = pl.pallas_call(
        hand_over,
        name="outputs",
        out_shape=(
            jax.ShapeDtypeStruct((TOKENS, SHARE), BF),
            jax.ShapeDtypeStruct((TOKENS, GROUP), BF),
        ),
        in_specs=[vmem, vmem],
        out_specs=(vmem, vmem),
    )(updated, layer_two)
    return (
        updated.reshape(frames, tile_rows, tile_cols, SHARE),
        layer_two.reshape(frames, tile_rows, tile_cols, GROUP),
    )


def solution(mesh):
    in_specs = (
        P("tm", "row", None, None),
        P("tm", "row", None, None, "head"),
        P(("row", "tm"), "head"),
        P(),
        P(("row", "tm"), None, "head"),
    )
    out_specs = (P("tm", "row", None, "head"), P("tm", "row", None, "head"))
    return jax.shard_map(shards, mesh=mesh, in_specs=in_specs, out_specs=out_specs, check_vma=False)
```
